128 devices in a mesh: tx: 8 (over x, y_hi), ty: 16 (over z, y_lo, core).
Axes of the slice: x: 4, y: 4 (y_hi: 2, y_lo: 2; y = y_hi * 2 + y_lo), z: 4, core: 2. Of those that a mesh axis runs over, the one named last changes fastest.
Arguments:
- seed_fluid: float32 [64, 512, 1024], P('ty', 'tx'), may hold values from -6 to 6
- seed_plate: float32 [16, 512, 1024], P(None, 'ty', 'tx'), may hold values from -6 to 6
- velocity: bfloat16 [4, 3, 64, 512, 1024], P(None, None, 'ty', 'tx'), may hold values from -4 to 4
- enthalpy: float32 [4, 16, 512, 1024], P(None, None, 'ty', 'tx'), may hold values from 0 to 1
- phase: int32 [4, 16, 512, 1024], P(None, None, 'ty', 'tx'), may hold values from 0 to 2
- contact: int32 [512, 1024], P('ty', 'tx'), may hold values 0 or 1
Outputs:
- adjoint_fluid: float32 [64, 512, 1024], P('ty', 'tx')
- adjoint_plate: float32 [16, 512, 1024], P(None, 'ty', 'tx')
The draws below stay inside these ranges and needn't reach their ends.
All inputs are finite; a program needn't handle non-finite values. No bound on the sum of `contact` on one device may be relied on, other than what follows from the above.
Results may differ from the reference program's by a relative error of at most 0.0003.
Values sent between devices are 32-bit elements; how exact they have to be, the bound alone decides.
A program may use at most 128 MiB of HBM per device.

```python
import jax
import jax.numpy as jnp
from jax import lax

PZ = 16
STEPS = 4
NX = 1024
NY = 512
FZ = 64


def place_ends(array, key, least, top_value):
    longest = array.shape.index(max(array.shape))
    spots = []
    for shift in (0, 1):
        where = [jax.random.randint(jax.random.fold_in(key, axis), (), 0, length) for axis, length in enumerate(array.shape)]
        where[longest] = (where[longest] + shift) % array.shape[longest]
        spots.append(tuple(where))
    return array.at[spots[0]].set(least).at[spots[1]].set(top_value)


def levels(key, dims, shards, low, high):
    loudness = 1.0
    for dim, blocks in shards:
        draws = jax.random.uniform(jax.random.fold_in(jax.random.fold_in(key, 6), dim), (blocks,), jnp.float32, low / len(shards), high / len(shards))
        loudness = loudness * jnp.repeat(jnp.exp(draws), dims[dim] // blocks).reshape((-1,) + (1,) * (len(dims) - 1 - dim))
    return loudness


def scatter_about(stream_key, extent, spread, most, pieces=(), dtype=jnp.bfloat16):
    level = levels(stream_key, extent, pieces, -0.22, 0.18) if pieces else 1.0
    entries = jax.random.normal(stream_key, extent, jnp.float32) * spread * level
    return jnp.minimum(jnp.maximum(entries, -most), most).astype(dtype)


def setup_inputs(seed: int = 0) -> dict:
    seeds = jax.random.split(jax.random.key(seed), 7)
    seed_fluid = scatter_about(seeds[0], (FZ, NY, NX), 1.0, 6.0, ((0, 16), (1, 8)), jnp.float32)
    seed_plate = scatter_about(seeds[1], (PZ, NY, NX), 1.0, 6.0, ((1, 16), (2, 8)), jnp.float32)
    velocity = scatter_about(seeds[2], (STEPS, 3, FZ, NY, NX), 1.0, 4.0, ((2, 16), (3, 8)))
    enthalpy = jnp.clip(1.0 * jax.random.uniform(seeds[3], (STEPS, PZ, NY, NX), jnp.float32) ** levels(seeds[3], (STEPS, PZ, NY, NX), ((2, 16), (3, 8)), -0.2, 0.2), 0.0, 1.0)
    phase = place_ends(jax.random.randint(seeds[4], (STEPS, PZ, NY, NX), 0, 3), jax.random.fold_in(seeds[4], 1), 0, 2).astype(jnp.int32)
    contact = place_ends((jax.random.randint(seeds[5], (NY, NX), 0, 4) < 3).astype(jnp.int32), jax.random.fold_in(seeds[5], 1), 0, 1)
    return dict(seed_fluid=seed_fluid, seed_plate=seed_plate, velocity=velocity, enthalpy=enthalpy, phase=phase, contact=contact)


DIFFUSION = 0.1
ADVECTION = 0.2
PLATE_DIFFUSION = 0.12
FLUID_COUPLING = 0.5
PLATE_COUPLING = 0.5


def laplace(field):
    padded = jnp.pad(field, 1)
    summed = padded[2:, 1:-1, 1:-1] + padded[:-2, 1:-1, 1:-1]
    summed = summed + padded[1:-1, 2:, 1:-1] + padded[1:-1, :-2, 1:-1]
    summed = summed + padded[1:-1, 1:-1, 2:] + padded[1:-1, 1:-1, :-2]
    return summed - 6.0 * field


def central(field, dimension):
    widths = [(0, 0), (0, 0), (0, 0)]
    widths[dimension] = (1, 1)
    padded = jnp.pad(field, widths)
    length = field.shape[dimension]
    upper = lax.slice_in_dim(padded, 2, length + 2, axis=dimension)
    lower = lax.slice_in_dim(padded, 0, length, axis=dimension)
    return 0.5 * (upper - lower)


def phase_slopes(states, saved):
    mushy = 1.0 / (1.0 + 8.0 * saved * (1.0 - saved))
    return jnp.where(states == 0, 1.0, jnp.where(states == 2, 0.7, mushy))


def reference(seed_fluid, seed_plate, velocity, enthalpy, phase, contact):
    adjoint_fluid = seed_fluid
    adjoint_plate = seed_plate
    contact_map = contact.astype(jnp.float32)
    for step in reversed(range(STEPS)):
        speed_x = velocity[step, 0].astype(jnp.float32)
        speed_y = velocity[step, 1].astype(jnp.float32)
        speed_z = velocity[step, 2].astype(jnp.float32)
        coupling = contact_map * (PLATE_COUPLING * adjoint_plate[-1] - FLUID_COUPLING * adjoint_fluid[0])
        advected = central(speed_x * adjoint_fluid, 2) + central(speed_y * adjoint_fluid, 1) + central(speed_z * adjoint_fluid, 0)
        fluid_next = adjoint_fluid + DIFFUSION * laplace(adjoint_fluid) + ADVECTION * advected
        fluid_next = fluid_next.at[0].add(coupling)
        slopes = phase_slopes(phase[step], enthalpy[step])
        forcing = PLATE_DIFFUSION * laplace(adjoint_plate)
        forcing = forcing.at[-1].add(-coupling)
        adjoint_plate = adjoint_plate + slopes * forcing
        adjoint_fluid = fluid_next
    return adjoint_fluid, adjoint_plate
```

```python
import jax
import jax.numpy as jnp
from jax import lax
from jax.experimental import pallas as pl
from jax.experimental.pallas import tpu as pltpu
from jax.sharding import PartitionSpec as P

MESH = pl.DeviceIdType.MESH
STEPS = 4
PZ = 16
LAYERS = 4
ROWS = 64
BLOCKS = 8
CHUNKS = 4
PROWS = 32
LANES = 128
TX = 8
TY = 16


def kernel(
    seed_fluid, seed_plate, velocity, enthalpy, phase, contact,
    out_fluid, out_plate,
    F, V, ZS, ZR, YS, YR, CR, CC, CF, CI, PR, PT, EN, PH, PYS, PYR, PXS, PXR, SXM,
    load_f, load_v, load_p, load_e, out_sem,
    zs_sem, zr_sem, ys_sem, yr_sem, cs_sem, cr_sem, ccs_sem, ccr_sem, fs_sem, pr_sem,
    pys_sem, pyr_sem, pxs_sem, pxr_sem,
):
    tx = lax.axis_index("tx")
    ty = lax.axis_index("ty")
    has_down, has_up = ty > 0, ty < TY - 1
    has_lo, has_hi = tx > 0, tx < TX - 1
    is_wall = ty == 0
    home_tx = ty // 2
    is_self = (tx == 0) & (ty == 0)
    not_self = jnp.logical_not(is_self)
    lane = lax.broadcasted_iota(jnp.int32, (ROWS, LANES), 1)
    row = lax.broadcasted_iota(jnp.int32, (ROWS, LANES), 0)

    def lanes(b):
        return pl.ds(pl.multiple_of(b * LANES, LANES), LANES)

    f_loads = [
        pltpu.make_async_copy(seed_fluid.at[:, :, pl.ds(b * LANES, LANES)], F.at[0, b], load_f.at[b])
        for b in range(BLOCKS)
    ]
    for copy in f_loads:
        copy.start()
    for c in (2, 1, 0):
        pltpu.make_async_copy(velocity.at[STEPS - 1, c], V.at[STEPS - 1, c], load_v.at[STEPS - 1, c]).start()
    contact_load = pltpu.make_async_copy(contact, CI, load_p.at[1])
    contact_load.start()
    plate_load = pltpu.make_async_copy(seed_plate, PT.at[0], load_p.at[0])
    plate_load.start()

    def late_loads(n):
        e = pltpu.make_async_copy(enthalpy.at[n], EN.at[n], load_e.at[n, 0])
        p = pltpu.make_async_copy(phase.at[n], PH.at[n], load_e.at[n, 1])
        v = [pltpu.make_async_copy(velocity.at[n, c], V.at[n, c], load_v.at[n, c]) for c in range(3)]
        return e, p, v

    barrier = pltpu.get_barrier_semaphore()

    def greet(cond, device):
        @pl.when(cond)
        def _():
            pl.semaphore_signal(barrier, inc=1, device_id=device, device_id_type=MESH)

        return jnp.where(cond, 1, 0)

    expected = greet(not_self, (home_tx, 0))
    for c in range(TX):
        for r in range(2):
            expected += greet(is_wall & ((tx > 0) | (2 * c + r > 0)), (c, 2 * tx + r))
    expected += greet(has_lo, (tx - 1, ty))
    expected += greet(has_hi, (tx + 1, ty))
    expected += greet(has_down, (tx, ty - 1))
    expected += greet(has_up, (tx, ty + 1))

    for n in (3, 2, 1, 0):
        e, p, v = late_loads(n)
        e.start()
        p.start()
        if n < STEPS - 1:
            for copy in v:
                copy.start()

    def remote(src, dst, send, recv, device):
        return pltpu.make_async_remote_copy(
            src_ref=src, dst_ref=dst, send_sem=send, recv_sem=recv, device_id=device, device_id_type=MESH
        )

    def z_down(s, j):
        blocks = pl.ds(2 * j, 2)
        return remote(ZS.at[s, 0, blocks], ZR.at[s, 1, blocks], zs_sem.at[s, 0, j], zr_sem.at[s, 1, j], (tx, ty - 1))

    def z_up(s, j):
        blocks = pl.ds(2 * j, 2)
        return remote(ZS.at[s, 1, blocks], ZR.at[s, 0, blocks], zs_sem.at[s, 1, j], zr_sem.at[s, 0, j], (tx, ty + 1))

    def y_lo(s, j):
        return remote(YS.at[s, 0, j], YR.at[s, 1, j], ys_sem.at[s, 0, j], yr_sem.at[s, 1, j], (tx - 1, ty))

    def y_hi(s, j):
        return remote(YS.at[s, 1, j], YR.at[s, 0, j], ys_sem.at[s, 1, j], yr_sem.at[s, 0, j], (tx + 1, ty))

    def wall_out(s, j, bb, r):
        b = 2 * j + bb
        return remote(
            F.at[s, b, 0, pl.ds(PROWS * r, PROWS)], PR.at[s], fs_sem.at[s, b, r], pr_sem.at[s], (b, 2 * tx + r)
        )

    def each_wall_out(s, j, act):
        for bb in range(2):
            for r in range(2):
                away = is_wall if (bb, r) != (0, 0) else is_wall & ((tx > 0) | (j > 0))

                @pl.when(away)
                def _(bb=bb, r=r):
                    act(wall_out(s, j, bb, r))

    def launch(s, j):
        pl.when(has_lo)(lambda: y_lo(s, j).start())
        pl.when(has_hi)(lambda: y_hi(s, j).start())
        pl.when(has_down)(lambda: z_down(s, j).start())
        pl.when(has_up)(lambda: z_up(s, j).start())
        each_wall_out(s, j, lambda copy: copy.start())

        @pl.when(is_self & (j == 0))
        def _():
            pltpu.make_async_copy(F.at[s, 0, 0, pl.ds(0, PROWS)], PR.at[s], pr_sem.at[s]).start()

    def sent(s, j):
        pl.when(has_lo)(lambda: y_lo(s, j).wait_send())
        pl.when(has_hi)(lambda: y_hi(s, j).wait_send())
        pl.when(has_down)(lambda: z_down(s, j).wait_send())
        pl.when(has_up)(lambda: z_up(s, j).wait_send())
        each_wall_out(s, j, lambda copy: copy.wait_send())

    def stage(s, j):
        n = STEPS - 1 - s
        for bb in range(2):
            b = 2 * j + bb
            g = 0.1 * F[s, b, 0]
            ZS[s, 0, b] = g + g * V[n, 2, 0, :, lanes(b)].astype(jnp.float32)
            g = 0.1 * F[s, b, LAYERS - 1]
            ZS[s, 1, b] = g - g * V[n, 2, LAYERS - 1, :, lanes(b)].astype(jnp.float32)
            for l in range(LAYERS):
                q = LAYERS * bb + l
                g = 0.1 * F[s, b, l, 0:1, :]
                v = V[n, 1, l, 0:16, lanes(b)].astype(jnp.float32)[0:1]
                YS[s, 0, j, q : q + 1, :] = g + g * v
                g = 0.1 * F[s, b, l, ROWS - 1 : ROWS, :]
                v = V[n, 1, l, ROWS - 16 : ROWS, lanes(b)].astype(jnp.float32)[15:16]
                YS[s, 1, j, q : q + 1, :] = g - g * v

    def interior(s, b):
        n = STEPS - 1 - s
        before = jnp.maximum(b - 1, 0)
        pending = below = None
        for l in range(LAYERS):
            f = F[s, b, l]
            g = 0.1 * f
            gu = g * V[n, 0, l, :, lanes(b)].astype(jnp.float32)
            gv = g * V[n, 1, l, :, lanes(b)].astype(jnp.float32)
            gw = g * V[n, 2, l, :, lanes(b)].astype(jnp.float32)
            from_right = pltpu.roll(g + gu, LANES - 1, 1)
            from_left = pltpu.roll(g - gu, 1, 1)
            from_above = pltpu.roll(g + gv, ROWS - 1, 0)
            from_below = pltpu.roll(g - gv, 1, 0)
            total = 0.4 * f
            total += jnp.where(lane == LANES - 1, 0.0, from_right)
            total += jnp.where(lane == 0, jnp.where(b > 0, SXM[l], 0.0), from_left)
            total += jnp.where(row == ROWS - 1, 0.0, from_above)
            total += jnp.where(row == 0, 0.0, from_below)
            SXM[l] = from_left
            if l > 0:
                F[s + 1, b, l - 1] = pending + (g + gw)
                total += below
            below = g - gw
            pending = total
            edge = jnp.where((lane == LANES - 1) & (b > 0), from_right, 0.0)
            if l > 0:
                F[s + 1, before, l - 1] += edge_before
            edge_before = edge
        F[s + 1, b, LAYERS - 1] = pending
        F[s + 1, before, LAYERS - 1] += edge_before

    def finish(s, j):
        @pl.when(has_lo)
        def _():
            y_hi(s, j).wait_recv()
            for q in range(2 * LAYERS):
                b, l = 2 * j + q // LAYERS, q % LAYERS
                F[s + 1, b, l, 0:1, :] += YR[s, 0, j, q : q + 1, :]

        @pl.when(has_hi)
        def _():
            y_lo(s, j).wait_recv()
            for q in range(2 * LAYERS):
                b, l = 2 * j + q // LAYERS, q % LAYERS
                F[s + 1, b, l, ROWS - 1 : ROWS, :] += YR[s, 1, j, q : q + 1, :]

        @pl.when(has_down)
        def _():
            z_up(s, j).wait_recv()
            for bb in range(2):
                F[s + 1, 2 * j + bb, 0] += ZR[s, 0, 2 * j + bb]

        @pl.when(has_up)
        def _():
            z_down(s, j).wait_recv()
            for bb in range(2):
                F[s + 1, 2 * j + bb, LAYERS - 1] += ZR[s, 1, 2 * j + bb]

        @pl.when(is_wall)
        def _():
            blocks = pl.ds(2 * j, 2)
            pltpu.make_async_copy(CR.at[s, blocks], CR.at[s, blocks], cr_sem.at[s, j]).wait()

            @pl.when(s == 0)
            def _():
                pltpu.make_async_copy(CC.at[blocks], CC.at[blocks], ccr_sem.at[j]).wait()

            for bb in range(2):
                b = 2 * j + bb
                F[s + 1, b, 0] += CC[b] * (0.5 * CR[s, b] - 0.5 * F[s, b, 0])

    tile_rows = pl.ds(pl.multiple_of(PROWS * lax.rem(ty, 2), PROWS), PROWS)
    tile_chunk = tx // 2

    def wall_in(s):
        return remote(
            PT.at[s, PZ - 1], CR.at[s, tx, tile_rows], cs_sem.at[s], cr_sem.at[s, tile_chunk], (home_tx, 0)
        )

    def contact_in():
        return remote(CF, CC.at[tx, tile_rows], ccs_sem.at[0], ccr_sem.at[tile_chunk], (home_tx, 0))

    def py_lo(s):
        return remote(PYS.at[s, 0], PYR.at[s, 1], pys_sem.at[s, 0], pyr_sem.at[s, 1], (tx, ty - 1))

    def py_hi(s):
        return remote(PYS.at[s, 1], PYR.at[s, 0], pys_sem.at[s, 1], pyr_sem.at[s, 0], (tx, ty + 1))

    def px_lo(s):
        return remote(PXS.at[s], PXR.at[s, 1], pxs_sem.at[s, 0], pxr_sem.at[s, 1], (tx - 1, ty))

    def px_hi(s):
        return remote(PXS.at[s], PXR.at[s, 0], pxs_sem.at[s, 1], pxr_sem.at[s, 0], (tx + 1, ty))

    def plate_launch(s):
        pl.when(not_self)(lambda: wall_in(s).start())

        @pl.when(is_self)
        def _():
            pltpu.make_async_copy(PT.at[s, PZ - 1], CR.at[s, 0, pl.ds(0, PROWS)], cr_sem.at[s, 0]).start()

        pl.when(has_lo)(lambda: px_lo(s).start())
        pl.when(has_hi)(lambda: px_hi(s).start())
        pl.when(has_down)(lambda: py_lo(s).start())
        pl.when(has_up)(lambda: py_hi(s).start())

    def plate_sent(s):
        pl.when(not_self)(lambda: wall_in(s).wait_send())
        pl.when(has_lo)(lambda: px_lo(s).wait_send())
        pl.when(has_hi)(lambda: px_hi(s).wait_send())
        pl.when(has_down)(lambda: py_lo(s).wait_send())
        pl.when(has_up)(lambda: py_hi(s).wait_send())

    small_lane = lax.broadcasted_iota(jnp.int32, (8, LANES), 1)

    def edge_rows(s, z, value):
        PYS[s, 0, pl.ds(z, 1), :] = value[0:1]
        PYS[s, 1, pl.ds(z, 1), :] = value[PROWS - 1 : PROWS]

    def edge_columns(packed, z, value):
        for k in range(PROWS // 8):
            part = value[8 * k : 8 * k + 8]
            place = 16 * k + z
            packed = jnp.where(small_lane == place, pltpu.roll(part, place, 1), packed)
            packed = jnp.where(small_lane == place + 64, pltpu.roll(part, place + 65, 1), packed)
        return packed

    def plate_stage(s):
        def body(z, packed):
            value = PT[s, z]
            edge_rows(s, z, value)
            return edge_columns(packed, z, value)

        PXS[s] = lax.fori_loop(0, PZ, body, jnp.zeros((8, LANES), jnp.float32))

    plate_lane = lax.broadcasted_iota(jnp.int32, (PROWS, LANES), 1)
    plate_row = lax.broadcasted_iota(jnp.int32, (PROWS, LANES), 0)

    def plate_step(s):
        n = STEPS - 1 - s
        pltpu.make_async_copy(PR.at[s], PR.at[s], pr_sem.at[s]).wait()
        pl.when(has_lo)(lambda: px_hi(s).wait_recv())
        pl.when(has_hi)(lambda: px_lo(s).wait_recv())
        pl.when(has_down)(lambda: py_hi(s).wait_recv())
        pl.when(has_up)(lambda: py_lo(s).wait_recv())
        e, p, _ = late_loads(n)
        e.wait()
        p.wait()
        from_lo, from_hi = PXR[s, 0], PXR[s, 1]
        coupling = CF[...] * (0.5 * PT[s, PZ - 1] - 0.5 * PR[s])

        def body(z, packed):
            value = PT[s, z]
            left = [pltpu.roll(from_lo, 64 - 16 * k - z, 1) for k in range(PROWS // 8)]
            right = [pltpu.roll(from_hi, LANES - 1 - 16 * k - z, 1) for k in range(PROWS // 8)]
            total = jnp.where(plate_lane == 0, jnp.concatenate(left, 0), pltpu.roll(value, 1, 1))
            total += jnp.where(
                plate_lane == LANES - 1, jnp.concatenate(right, 0), pltpu.roll(value, LANES - 1, 1)
            )
            total += jnp.where(plate_row == 0, PYR[s, 0, pl.ds(z, 1), :], pltpu.roll(value, 1, 0))
            total += jnp.where(
                plate_row == PROWS - 1, PYR[s, 1, pl.ds(z, 1), :], pltpu.roll(value, PROWS - 1, 0)
            )
            total += jnp.where(z > 0, PT[s, jnp.maximum(z - 1, 0)], 0.0)
            total += jnp.where(z < PZ - 1, PT[s, jnp.minimum(z + 1, PZ - 1)], 0.0)
            forcing = 0.12 * (total - 6.0 * value) - jnp.where(z == PZ - 1, coupling, 0.0)
            saved = EN[n, z]
            state = PH[n, z]
            slopes = 1.0 / (1.0 + 8.0 * saved * (1.0 - saved))
            slopes = jnp.where(state == 0, 1.0, jnp.where(state == 2, 0.7, slopes))
            value = value + slopes * forcing
            PT[s + 1, z] = value
            edge_rows(s + 1, z, value)
            return edge_columns(packed, z, value)

        packed = lax.fori_loop(0, PZ, body, jnp.zeros((8, LANES), jnp.float32))

        @pl.when(s < STEPS - 1)
        def _():
            PXS[s + 1] = packed
            plate_launch(s + 1)

        plate_sent(s)

        @pl.when(s == STEPS - 1)
        def _():
            pltpu.make_async_copy(PT.at[STEPS], out_plate, out_sem.at[CHUNKS]).start()

    for absent, side in ((ty == 0, 0), (ty == TY - 1, 1)):
        @pl.when(absent)
        def _(side=side):
            for s in range(STEPS):
                PYR[s, side] = jnp.zeros((PZ, LANES), jnp.float32)

    for absent, side in ((tx == 0, 0), (tx == TX - 1, 1)):
        @pl.when(absent)
        def _(side=side):
            for s in range(STEPS):
                PXR[s, side] = jnp.zeros((8, LANES), jnp.float32)

    contact_load.wait()
    CF[...] = CI[...].astype(jnp.float32)
    for copy in f_loads:
        copy.wait()
    for c in (2, 1, 0):
        pltpu.make_async_copy(velocity.at[STEPS - 1, c], V.at[STEPS - 1, c], load_v.at[STEPS - 1, c]).wait()

    def first_stage(j, carry):
        stage(0, j)
        return carry

    lax.fori_loop(0, CHUNKS, first_stage, 0)
    plate_load.wait()
    plate_stage(0)
    pl.semaphore_wait(barrier, expected)

    pl.when(not_self)(lambda: contact_in().start())

    @pl.when(is_self)
    def _():
        pltpu.make_async_copy(CF, CC.at[0, pl.ds(0, PROWS)], ccr_sem.at[0]).start()

    plate_launch(0)

    def first_launch(j, carry):
        launch(0, j)
        return carry

    lax.fori_loop(0, CHUNKS, first_launch, 0)

    def first_interior(b, carry):
        interior(0, b)
        return carry

    lax.fori_loop(0, BLOCKS, first_interior, 0)

    def slot(t, carry):
        s, j = t // CHUNKS, lax.rem(t, CHUNKS)
        finish(s, j)

        @pl.when(s < STEPS - 1)
        def _():
            @pl.when(j == 0)
            def _():
                for copy in late_loads(STEPS - 2 - s)[2]:
                    copy.wait()

            stage(s + 1, j)
            launch(s + 1, j)

            def body(bb, c):
                interior(s + 1, 2 * j + bb)
                return c

            lax.fori_loop(0, 2, body, 0)

        @pl.when(s == STEPS - 1)
        def _():
            where = pl.ds(pl.multiple_of(2 * LANES * j, 2 * LANES), 2 * LANES)
            for bb in range(2):
                b = 2 * j + bb
                pltpu.make_async_copy(F.at[STEPS, b], out_fluid.at[:, :, lanes(b)], out_sem.at[j]).start()

        sent(s, j)
        for step in range(STEPS):
            @pl.when(t == jnp.maximum(CHUNKS * step + tile_chunk - 1, 1))
            def _(step=step):
                plate_step(step)

        return carry

    lax.fori_loop(0, STEPS * CHUNKS, slot, 0)

    pl.when(not_self)(lambda: contact_in().wait_send())
    for j in range(CHUNKS):
        pltpu.make_async_copy(F.at[STEPS, pl.ds(2 * j, 2)], F.at[STEPS, pl.ds(2 * j, 2)], out_sem.at[j]).wait()
    pltpu.make_async_copy(PT.at[STEPS], out_plate, out_sem.at[CHUNKS]).wait()


def on_device(seed_fluid, seed_plate, velocity, enthalpy, phase, contact):
    f32 = jnp.float32
    dma = pltpu.SemaphoreType.DMA
    return pl.pallas_call(
        kernel,
        out_shape=(
            jax.ShapeDtypeStruct(seed_fluid.shape, f32),
            jax.ShapeDtypeStruct(seed_plate.shape, f32),
        ),
        in_specs=[pl.BlockSpec(memory_space=pl.ANY)] * 6,
        out_specs=(pl.BlockSpec(memory_space=pl.ANY),) * 2,
        scratch_shapes=[
            pltpu.VMEM((STEPS + 1, BLOCKS, LAYERS, ROWS, LANES), f32),
            pltpu.VMEM((STEPS, 3, LAYERS, ROWS, BLOCKS * LANES), jnp.bfloat16),
            pltpu.VMEM((STEPS, 2, BLOCKS, ROWS, LANES), f32),
            pltpu.VMEM((STEPS, 2, BLOCKS, ROWS, LANES), f32),
            pltpu.VMEM((STEPS, 2, CHUNKS, 2 * LAYERS, LANES), f32),
            pltpu.VMEM((STEPS, 2, CHUNKS, 2 * LAYERS, LANES), f32),
            pltpu.VMEM((STEPS, BLOCKS, ROWS, LANES), f32),
            pltpu.VMEM((BLOCKS, ROWS, LANES), f32),
            pltpu.VMEM((PROWS, LANES), f32),
            pltpu.VMEM((PROWS, LANES), jnp.int32),
            pltpu.VMEM((STEPS, PROWS, LANES), f32),
            pltpu.VMEM((STEPS + 1, PZ, PROWS, LANES), f32),
            pltpu.VMEM((STEPS, PZ, PROWS, LANES), f32),
            pltpu.VMEM((STEPS, PZ, PROWS, LANES), jnp.int32),
            pltpu.VMEM((STEPS + 1, 2, PZ, LANES), f32),
            pltpu.VMEM((STEPS, 2, PZ, LANES), f32),
            pltpu.VMEM((STEPS, 8, LANES), f32),
            pltpu.VMEM((STEPS, 2, 8, LANES), f32),
            pltpu.VMEM((LAYERS, ROWS, LANES), f32),
            dma((BLOCKS,)),
            dma((STEPS, 3)),
            dma((2,)),
            dma((STEPS, 2)),
            dma((CHUNKS + 1,)),
            dma((STEPS, 2, CHUNKS)),
            dma((STEPS, 2, CHUNKS)),
            dma((STEPS, 2, CHUNKS)),
            dma((STEPS, 2, CHUNKS)),
            dma((STEPS,)),
            dma((STEPS, CHUNKS)),
            dma((1,)),
            dma((CHUNKS,)),
            dma((STEPS, BLOCKS, 2)),
            dma((STEPS,)),
            dma((STEPS, 2)),
            dma((STEPS, 2)),
            dma((STEPS, 2)),
            dma((STEPS, 2)),
        ],
        compiler_params=pltpu.CompilerParams(
            collective_id=0, has_side_effects=True, vmem_limit_bytes=48 * 1024 * 1024
        ),
        cost_estimate=pl.CostEstimate(flops=35_000_000, bytes_accessed=11_000_000, transcendentals=0),
    )(seed_fluid, seed_plate, velocity, enthalpy, phase, contact)


def solution(mesh):
    return jax.shard_map(
        on_device,
        mesh=mesh,
        in_specs=(
            P("ty", "tx", None),
            P(None, "ty", "tx"),
            P(None, None, "ty", "tx", None),
            P(None, None, "ty", "tx"),
            P(None, None, "ty", "tx"),
            P("ty", "tx"),
        ),
        out_specs=(P("ty", "tx", None), P(None, "ty", "tx")),
        check_vma=False,
    )
```

```python
import jax
import jax.numpy as jnp
from jax import lax
from jax.experimental import pallas as pl
from jax.experimental.pallas import tpu as pltpu
from jax.sharding import PartitionSpec as P

MESH = pl.DeviceIdType.MESH
STEPS = 4
PZ = 16
LAYERS = 4
ROWS = 64
BLOCKS = 8
CHUNKS = 4
PROWS = 32
LANES = 128
PLATE_SLOTS = ((0, 5), (1, 8), (2, 11), (3, 15))
CARRY_SLOTS = ((1, 8), (2, 12), (3, 15))
COUPLE_SLOTS = ((0, 5), (1, 10), (2, 12), (3, 15))
TX = 8
TY = 16


def kernel(
    seed_fluid, seed_plate, velocity, enthalpy, phase, contact,
    out_fluid, out_plate,
    F, NF, V, ZS, ZR, YS, YR, CR, CC, CF, CI, PR, PT, NP, TOP, EN, PH, SL, PYS, PYR, PXS, PXR, SXM, SXP, AS, AM, CP, D, ND, DXM, DXP, DYS, DYR,
    load_f, load_v, load_p, load_e, out_sem,
    zs_sem, zr_sem, ys_sem, yr_sem, cs_sem, cr_sem, ccs_sem, ccr_sem, fs_sem, pr_sem,
    pys_sem, pyr_sem, pxs_sem, pxr_sem, dys_sem, dyr_sem,
):
    tx = lax.axis_index("tx")
    ty = lax.axis_index("ty")
    has_down, has_up = ty > 0, ty < TY - 1
    has_lo, has_hi = tx > 0, tx < TX - 1
    is_wall = ty == 0
    home_tx = ty // 2
    is_self = (tx == 0) & (ty == 0)
    not_self = jnp.logical_not(is_self)
    lane = lax.broadcasted_iota(jnp.int32, (ROWS, LANES), 1)
    row = lax.broadcasted_iota(jnp.int32, (ROWS, LANES), 0)

    def lanes(b):
        return pl.ds(pl.multiple_of(b * LANES, LANES), LANES)

    f_loads = [
        pltpu.make_async_copy(seed_fluid.at[:, :, pl.ds(b * LANES, LANES)], F.at[b], load_f.at[b])
        for b in range(BLOCKS)
    ]
    for copy in f_loads:
        copy.start()
    for c in (2, 1, 0):
        pltpu.make_async_copy(velocity.at[STEPS - 1, c], V.at[STEPS - 1, c], load_v.at[STEPS - 1, c]).start()
    contact_load = pltpu.make_async_copy(contact, CI, load_p.at[1])
    contact_load.start()
    plate_load = pltpu.make_async_copy(seed_plate, PT, load_p.at[0])
    plate_load.start()

    def late_loads(n):
        e = pltpu.make_async_copy(enthalpy.at[n], EN.at[n], load_e.at[n, 0])
        p = pltpu.make_async_copy(phase.at[n], PH.at[n], load_e.at[n, 1])
        v = [pltpu.make_async_copy(velocity.at[n, c], V.at[n, c], load_v.at[n, c]) for c in range(3)]
        return e, p, v

    barrier = pltpu.get_barrier_semaphore()

    def greet(cond, device):
        @pl.when(cond)
        def _():
            pl.semaphore_signal(barrier, inc=1, device_id=device, device_id_type=MESH)

        return jnp.where(cond, 1, 0)

    expected = greet(not_self, (home_tx, 0))
    expected += greet(has_lo, (tx - 1, ty))
    expected += greet(has_hi, (tx + 1, ty))
    expected += greet(has_down, (tx, ty - 1))
    expected += greet(has_up, (tx, ty + 1))

    @pl.when(is_wall)
    def _():
        for c in range(TX):
            for r in range(2):
                greet((tx > 0) | (2 * c + r > 0), (c, 2 * tx + r))

    expected += jnp.where(is_wall, jnp.where(is_self, 15, 16), 0)

    for n in (3, 2, 1, 0):
        e, p, v = late_loads(n)
        e.start()
        p.start()
        if n < STEPS - 1:
            for copy in v:
                copy.start()

    def remote(src, dst, send, recv, device):
        return pltpu.make_async_remote_copy(
            src_ref=src, dst_ref=dst, send_sem=send, recv_sem=recv, device_id=device, device_id_type=MESH
        )

    def z_down(s, j):
        blocks = pl.ds(2 * j, 2)
        return remote(ZS.at[s, 0, blocks], ZR.at[s, 1, blocks], zs_sem.at[s, 0, j], zr_sem.at[s, 1, j], (tx, ty - 1))

    def z_up(s, j):
        blocks = pl.ds(2 * j, 2)
        return remote(ZS.at[s, 1, blocks], ZR.at[s, 0, blocks], zs_sem.at[s, 1, j], zr_sem.at[s, 0, j], (tx, ty + 1))

    def y_lo(s, j):
        return remote(YS.at[s, 0, j], YR.at[s, 1, j], ys_sem.at[s, 0, j], yr_sem.at[s, 1, j], (tx - 1, ty))

    def y_hi(s, j):
        return remote(YS.at[s, 1, j], YR.at[s, 0, j], ys_sem.at[s, 1, j], yr_sem.at[s, 0, j], (tx + 1, ty))

    def wall_out(s, j, bb, r):
        b = 2 * j + bb
        return remote(
            AM.at[s, b, pl.ds(PROWS * r, PROWS)], PR.at[s], fs_sem.at[s, b, r], pr_sem.at[s], (b, 2 * tx + r)
        )

    def each_wall_out(s, j, act):
        for bb in range(2):
            for r in range(2):
                away = is_wall if (bb, r) != (0, 0) else is_wall & ((tx > 0) | (j > 0))

                @pl.when(away)
                def _(bb=bb, r=r):
                    act(wall_out(s, j, bb, r))

    def launch_y(s, j):
        pl.when(has_lo)(lambda: y_lo(s, j).start())
        pl.when(has_hi)(lambda: y_hi(s, j).start())

    def launch_z(s, j):
        pl.when(has_down)(lambda: z_down(s, j).start())
        pl.when(has_up)(lambda: z_up(s, j).start())

    def wall_launch(s, j):
        each_wall_out(s, j, lambda copy: copy.start())

        @pl.when(is_self & (j == 0))
        def _():
            pltpu.make_async_copy(AM.at[s, 0, pl.ds(0, PROWS)], PR.at[s], pr_sem.at[s]).start()

    def sent(s, j):
        pl.when(has_lo)(lambda: y_lo(s, j).wait_send())
        pl.when(has_hi)(lambda: y_hi(s, j).wait_send())
        pl.when(has_down)(lambda: z_down(s, j).wait_send())
        pl.when(has_up)(lambda: z_up(s, j).wait_send())

    def stage_z(s, j):
        n = STEPS - 1 - s
        for bb in range(2):
            b = 2 * j + bb
            g = 0.1 * F[b, 0]
            ZS[s, 0, b] = g + g * V[n, 2, 0, :, lanes(b)].astype(jnp.float32)
            g = 0.1 * F[b, LAYERS - 1]
            ZS[s, 1, b] = g - g * V[n, 2, LAYERS - 1, :, lanes(b)].astype(jnp.float32)

    def stage_y(s, j, field, out):
        n = STEPS - 1 - s
        for q in range(2 * LAYERS):
            b, l = 2 * j + q // LAYERS, q % LAYERS
            g = 0.1 * field[b, l, 0:1, :]
            v = V[n, 1, l, 0:16, lanes(b)].astype(jnp.float32)[0:1]
            out[s, 0, j, q : q + 1, :] = g + g * v
            g = 0.1 * field[b, l, ROWS - 1 : ROWS, :]
            v = V[n, 1, l, ROWS - 16 : ROWS, lanes(b)].astype(jnp.float32)[15:16]
            out[s, 1, j, q : q + 1, :] = g - g * v

    def prime(s, field, xp, xm):
        for l in range(LAYERS):
            g = 0.1 * field[0, l]
            xp[l] = pltpu.roll(g + g * V[STEPS - 1 - s, 0, l, :, lanes(0)].astype(jnp.float32), LANES - 1, 1)
            xm[l] = jnp.zeros((ROWS, LANES), jnp.float32)

    def interior(s, b, field, out, xp, xm):
        n = STEPS - 1 - s
        after = jnp.minimum(b + 1, BLOCKS - 1)
        weight = jnp.where(b < BLOCKS - 1, 0.1, 0.0)
        pending = below = None
        for l in range(LAYERS):
            f = field[b, l]
            g = 0.1 * f
            gu = g * V[n, 0, l, :, lanes(b)].astype(jnp.float32)
            gv = g * V[n, 1, l, :, lanes(b)].astype(jnp.float32)
            gw = g * V[n, 2, l, :, lanes(b)].astype(jnp.float32)
            beyond = weight * field[after, l]
            beyond = beyond + beyond * V[n, 0, l, :, lanes(after)].astype(jnp.float32)
            from_beyond = pltpu.roll(beyond, LANES - 1, 1)
            from_left = pltpu.roll(g - gu, 1, 1)
            from_above = pltpu.roll(g + gv, ROWS - 1, 0)
            from_below = pltpu.roll(g - gv, 1, 0)
            total = 0.4 * f
            total += jnp.where(lane == LANES - 1, from_beyond, xp[l])
            total += jnp.where(lane == 0, xm[l], from_left)
            total += jnp.where(row == ROWS - 1, 0.0, from_above)
            total += jnp.where(row == 0, 0.0, from_below)
            xp[l] = from_beyond
            xm[l] = from_left
            if l > 0:
                out[b, l - 1] = pending + (g + gw)
                total += below
            below = g - gw
            pending = total
        out[b, LAYERS - 1] = pending

    def finish(s, j):
        @pl.when(has_lo)
        def _():
            y_hi(s, j).wait_recv()
            for q in range(2 * LAYERS):
                b, l = 2 * j + q // LAYERS, q % LAYERS
                NF[b, l, 0:1, :] += YR[s, 0, j, q : q + 1, :]

        @pl.when(has_hi)
        def _():
            y_lo(s, j).wait_recv()
            for q in range(2 * LAYERS):
                b, l = 2 * j + q // LAYERS, q % LAYERS
                NF[b, l, ROWS - 1 : ROWS, :] += YR[s, 1, j, q : q + 1, :]

        for bb in range(2):
            for l in range(1, LAYERS - 1):
                F[2 * j + bb, l] = NF[2 * j + bb, l]

        @pl.when(has_down)
        def _():
            z_up(s, j).wait_recv()
            for bb in range(2):
                F[2 * j + bb, 0] = NF[2 * j + bb, 0] + ZR[s, 0, 2 * j + bb]

        @pl.when(has_up)
        def _():
            z_down(s, j).wait_recv()
            for bb in range(2):
                F[2 * j + bb, LAYERS - 1] = NF[2 * j + bb, LAYERS - 1] + ZR[s, 1, 2 * j + bb]

        @pl.when(ty == TY - 1)
        def _():
            for bb in range(2):
                F[2 * j + bb, LAYERS - 1] = NF[2 * j + bb, LAYERS - 1]

        @pl.when(is_wall)
        def _():
            for bb in range(2):
                F[2 * j + bb, 0] = NF[2 * j + bb, 0]

            @pl.when(s < STEPS - 1)
            def _():
                for bb in range(2):
                    AS[s + 1, 2 * j + bb] = NF[2 * j + bb, 0]

            @pl.when(s == 0)
            def _():
                for bb in range(2):
                    AM[1, 2 * j + bb] = NF[2 * j + bb, 0]
                wall_launch(1, j)

    def d_lo(s):
        return remote(DYS.at[s, 0], DYR.at[s, 1], dys_sem.at[s, 0], dyr_sem.at[s, 1], (tx - 1, ty))

    def d_hi(s):
        return remote(DYS.at[s, 1], DYR.at[s, 0], dys_sem.at[s, 1], dyr_sem.at[s, 0], (tx + 1, ty))

    def carry_on(s):
        prime(s, D, DXP, DXM)

        def body(b, c):
            interior(s, b, D, ND, DXP, DXM)
            return c

        lax.fori_loop(0, BLOCKS, body, 0)
        for here, copy, side, at in ((has_lo, d_hi, 0, 0), (has_hi, d_lo, 1, ROWS - 1)):
            @pl.when(here)
            def _(copy=copy, side=side, at=at):
                copy(s).wait_recv()
                for b in range(BLOCKS):
                    for l in range(LAYERS):
                        q = LAYERS * (b % 2) + l
                        ND[b, l, at : at + 1, :] += DYR[s, side, b // 2, q : q + 1, :]

        pl.when(has_lo)(lambda: d_lo(s).wait_send())
        pl.when(has_hi)(lambda: d_hi(s).wait_send())

        @pl.when(s < STEPS - 1)
        def _():
            for b in range(BLOCKS):
                AM[s + 1, b] = AS[s + 1, b] + ND[b, 0]

            def body(j, c):
                wall_launch(s + 1, j)
                return c

            lax.fori_loop(0, CHUNKS, body, 0)

    def couple(s):
        for j in range(CHUNKS):
            blocks = pl.ds(2 * j, 2)
            pltpu.make_async_copy(CR.at[s, blocks], CR.at[s, blocks], cr_sem.at[s, j]).wait()

        @pl.when(s == 0)
        def _():
            for j in range(CHUNKS):
                blocks = pl.ds(2 * j, 2)
                pltpu.make_async_copy(CC.at[blocks], CC.at[blocks], ccr_sem.at[j]).wait()

        def body(b, c):
            wall = AS[s, b] + D[b, 0]
            D[b, 0] = ND[b, 0] + CC[b] * (0.5 * CR[s, b] - 0.5 * wall)
            for l in range(1, LAYERS):
                D[b, l] = ND[b, l]
            return c

        lax.fori_loop(0, BLOCKS, body, 0)

        @pl.when(s < STEPS - 1)
        def _():
            def body(j, c):
                stage_y(s + 1, j, D, DYS)
                return c

            lax.fori_loop(0, CHUNKS, body, 0)
            pl.when(has_lo)(lambda: d_lo(s + 1).start())
            pl.when(has_hi)(lambda: d_hi(s + 1).start())

        @pl.when(s == STEPS - 1)
        def _():
            def body(b, c):
                for l in range(LAYERS):
                    F[b, l] += D[b, l]
                return c

            lax.fori_loop(0, BLOCKS, body, 0)
            for j in range(CHUNKS):
                put_out(j)

    def put_out(j):
        for bb in range(2):
            b = 2 * j + bb
            pltpu.make_async_copy(F.at[b], out_fluid.at[:, :, lanes(b)], out_sem.at[j]).start()

    tile_rows = pl.ds(pl.multiple_of(PROWS * lax.rem(ty, 2), PROWS), PROWS)
    tile_chunk = tx // 2

    def wall_in(s):
        return remote(TOP.at[s], CR.at[s, tx, tile_rows], cs_sem.at[s], cr_sem.at[s, tile_chunk], (home_tx, 0))

    def contact_in():
        return remote(CF, CC.at[tx, tile_rows], ccs_sem.at[0], ccr_sem.at[tile_chunk], (home_tx, 0))

    def py_lo(s):
        return remote(PYS.at[s, 0], PYR.at[s, 1], pys_sem.at[s, 0], pyr_sem.at[s, 1], (tx, ty - 1))

    def py_hi(s):
        return remote(PYS.at[s, 1], PYR.at[s, 0], pys_sem.at[s, 1], pyr_sem.at[s, 0], (tx, ty + 1))

    def px_lo(s):
        return remote(PXS.at[s], PXR.at[s, 1], pxs_sem.at[s, 0], pxr_sem.at[s, 1], (tx - 1, ty))

    def px_hi(s):
        return remote(PXS.at[s], PXR.at[s, 0], pxs_sem.at[s, 1], pxr_sem.at[s, 0], (tx + 1, ty))

    def wall_reply(s):
        pl.when(not_self)(lambda: wall_in(s).start())

        @pl.when(is_self)
        def _():
            pltpu.make_async_copy(TOP.at[s], CR.at[s, 0, pl.ds(0, PROWS)], cr_sem.at[s, 0]).start()

    def plate_launch(s):
        pl.when(has_lo)(lambda: px_lo(s).start())
        pl.when(has_hi)(lambda: px_hi(s).start())
        pl.when(has_down)(lambda: py_lo(s).start())
        pl.when(has_up)(lambda: py_hi(s).start())

    def plate_sent(s):
        pl.when(not_self)(lambda: wall_in(s).wait_send())
        pl.when(has_lo)(lambda: px_lo(s).wait_send())
        pl.when(has_hi)(lambda: px_hi(s).wait_send())
        pl.when(has_down)(lambda: py_lo(s).wait_send())
        pl.when(has_up)(lambda: py_hi(s).wait_send())

    small_lane = lax.broadcasted_iota(jnp.int32, (8, LANES), 1)

    def edge_rows(s, z, value):
        PYS[s, 0, z : z + 1, :] = value[0:1]
        PYS[s, 1, z : z + 1, :] = value[PROWS - 1 : PROWS]

    def edge_columns(packed, z, value):
        for k in range(PROWS // 8):
            place = 2 * (16 * k + z)
            part = pltpu.roll(value[8 * k : 8 * k + 8], place + 1, 1)
            packed = jnp.where((small_lane == place) | (small_lane == place + 1), part, packed)
        return packed

    def merge(parts):
        while len(parts) > 1:
            parts = [x + y for x, y in zip(parts[::2], parts[1::2])]
        return parts[0]

    def plate_edges(s, plate):
        parts = []
        for z in range(PZ):
            value = plate[z]
            edge_rows(s, z, value)
            parts.append(edge_columns(jnp.zeros((8, LANES), jnp.float32), z, value))
        PXS[s] = merge(parts)

    plate_lane = lax.broadcasted_iota(jnp.int32, (PROWS, LANES), 1)
    plate_row = lax.broadcasted_iota(jnp.int32, (PROWS, LANES), 0)

    def slopes_of(n):
        e, p, _ = late_loads(n)
        e.wait()
        p.wait()
        for z in range(PZ):
            saved, state = EN[n, z], PH[n, z]
            slopes = 1.0 / (1.0 + 8.0 * saved * (1.0 - saved))
            SL[z] = jnp.where(state == 0, 1.0, jnp.where(state == 2, 0.7, slopes))

    def plate_step(s):
        @pl.when(s > 0)
        def _():
            for z in range(PZ):
                PT[z] = NP[z]

        pl.when(has_lo)(lambda: px_hi(s).wait_recv())
        pl.when(has_hi)(lambda: px_lo(s).wait_recv())
        pl.when(has_down)(lambda: py_hi(s).wait_recv())
        pl.when(has_up)(lambda: py_lo(s).wait_recv())
        beside = jnp.where(
            small_lane % 2 == 0, pltpu.roll(PXR[s, 1], LANES - 1, 1), pltpu.roll(PXR[s, 0], 1, 1)
        )
        for z in range(PZ):
            value = PT[z]
            ends = [pltpu.roll(beside, LANES - 1 - 2 * (16 * k + z), 1) for k in range(PROWS // 8)]
            ends = jnp.concatenate(ends, 0)
            total = jnp.where(plate_lane == 0, ends, pltpu.roll(value, 1, 1))
            total += jnp.where(plate_lane == LANES - 1, ends, pltpu.roll(value, LANES - 1, 1))
            total += jnp.where(plate_row == 0, PYR[s, 0, z : z + 1, :], pltpu.roll(value, 1, 0))
            total += jnp.where(plate_row == PROWS - 1, PYR[s, 1, z : z + 1, :], pltpu.roll(value, PROWS - 1, 0))
            if z > 0:
                total += PT[z - 1]
            if z < PZ - 1:
                total += PT[z + 1]
            NP[z] = value + SL[z] * (0.12 * (total - 6.0 * value))

    def plate_top(s):
        pltpu.make_async_copy(PR.at[s], PR.at[s], pr_sem.at[s]).wait()
        wall = PR[s] + jnp.where(s > 0, CP[...], 0.0)
        coupling = CF[...] * (0.5 * PT[PZ - 1] - 0.5 * wall)
        CP[...] = coupling
        value = NP[PZ - 1] - SL[PZ - 1] * coupling
        NP[PZ - 1] = value

        @pl.when(s < STEPS - 1)
        def _():
            TOP[s + 1] = value
            wall_reply(s + 1)
            plate_edges(s + 1, NP)
            plate_launch(s + 1)

        plate_sent(s)

        @pl.when(s < STEPS - 1)
        def _():
            slopes_of(STEPS - 2 - s)

        @pl.when(s == STEPS - 1)
        def _():
            pltpu.make_async_copy(NP, out_plate, out_sem.at[CHUNKS]).start()

    for absent, side in ((ty == 0, 0), (ty == TY - 1, 1)):
        @pl.when(absent)
        def _(side=side):
            for s in range(STEPS):
                PYR[s, side] = jnp.zeros((PZ, LANES), jnp.float32)

    for absent, side in ((tx == 0, 0), (tx == TX - 1, 1)):
        @pl.when(absent)
        def _(side=side):
            for s in range(STEPS):
                PXR[s, side] = jnp.zeros((8, LANES), jnp.float32)

    contact_load.wait()
    CF[...] = CI[...].astype(jnp.float32)
    for copy in f_loads:
        copy.wait()
    for c in (2, 1, 0):
        pltpu.make_async_copy(velocity.at[STEPS - 1, c], V.at[STEPS - 1, c], load_v.at[STEPS - 1, c]).wait()

    def first_stage(j, carry):
        stage_z(0, j)
        stage_y(0, j, F, YS)
        return carry

    lax.fori_loop(0, CHUNKS, first_stage, 0)

    @pl.when(is_wall)
    def _():
        for b in range(BLOCKS):
            AS[0, b] = F[b, 0]
            AM[0, b] = F[b, 0]
            for l in range(LAYERS):
                D[b, l] = jnp.zeros((ROWS, LANES), jnp.float32)
                ND[b, l] = jnp.zeros((ROWS, LANES), jnp.float32)

    plate_load.wait()
    TOP[0] = PT[PZ - 1]
    plate_edges(0, PT)
    pl.semaphore_wait(barrier, expected)

    def first_wall(chunk):
        @pl.when(tile_chunk == chunk)
        def _():
            wall_reply(0)
            pl.when(not_self)(lambda: contact_in().start())

            @pl.when(is_self)
            def _():
                pltpu.make_async_copy(CF, CC.at[0, pl.ds(0, PROWS)], ccr_sem.at[0]).start()

    first_wall(0)

    @pl.when(is_wall)
    def _():
        def body(j, carry):
            wall_launch(0, j)
            return carry

        lax.fori_loop(0, CHUNKS, body, 0)

    def first_launch(j, carry):
        launch_y(0, j)
        launch_z(0, j)
        return carry

    lax.fori_loop(0, CHUNKS, first_launch, 0)
    first_wall(1)
    plate_launch(0)

    def first_interior(b, carry):
        interior(0, b, F, NF, SXP, SXM)
        return carry

    prime(0, F, SXP, SXM)
    lax.fori_loop(0, BLOCKS // 2, first_interior, 0)
    first_wall(2)
    lax.fori_loop(BLOCKS // 2, BLOCKS, first_interior, 0)
    first_wall(3)
    slopes_of(STEPS - 1)

    def at(t, slots, act):
        due, s = False, 0
        for step, place in slots:
            due, s = due | (t == place), jnp.where(t == place, step, s)
        pl.when(due)(lambda: act(s))

    def plate(s):
        plate_step(s)
        plate_top(s)

    def slot(t, carry):
        s, j = t // CHUNKS, lax.rem(t, CHUNKS)
        finish(s, j)

        @pl.when(s < STEPS - 1)
        def _():
            @pl.when(j == 0)
            def _():
                for copy in late_loads(STEPS - 2 - s)[2]:
                    copy.wait()

            stage_z(s + 1, j)
            launch_z(s + 1, j)
            stage_y(s + 1, j, F, YS)
            launch_y(s + 1, j)

            @pl.when(j == 0)
            def _():
                prime(s + 1, F, SXP, SXM)

            def body(b, c):
                interior(s + 1, b, F, NF, SXP, SXM)
                return c

            lax.fori_loop(jnp.maximum(2 * j - 1, 0), jnp.where(j == CHUNKS - 1, BLOCKS, 2 * j + 1), body, 0)

        pl.when((s == STEPS - 1) & (ty > 0))(lambda: put_out(j))
        sent(s, j)

        @pl.when(is_wall)
        def _():
            at(t, CARRY_SLOTS, carry_on)
            at(t, COUPLE_SLOTS, couple)

        at(t, PLATE_SLOTS, plate)
        return carry

    lax.fori_loop(0, STEPS * CHUNKS, slot, 0)

    @pl.when(is_wall)
    def _():
        def body(t, c):
            each_wall_out(t // CHUNKS, lax.rem(t, CHUNKS), lambda copy: copy.wait_send())
            return c

        lax.fori_loop(0, STEPS * CHUNKS, body, 0)

    pl.when(not_self)(lambda: contact_in().wait_send())
    for j in range(CHUNKS):
        pltpu.make_async_copy(F.at[pl.ds(2 * j, 2)], F.at[pl.ds(2 * j, 2)], out_sem.at[j]).wait()
    pltpu.make_async_copy(NP, out_plate, out_sem.at[CHUNKS]).wait()


def on_device(seed_fluid, seed_plate, velocity, enthalpy, phase, contact):
    f32 = jnp.float32
    dma = pltpu.SemaphoreType.DMA
    return pl.pallas_call(
        kernel,
        out_shape=(
            jax.ShapeDtypeStruct(seed_fluid.shape, f32),
            jax.ShapeDtypeStruct(seed_plate.shape, f32),
        ),
        in_specs=[pl.BlockSpec(memory_space=pl.ANY)] * 6,
        out_specs=(pl.BlockSpec(memory_space=pl.ANY),) * 2,
        scratch_shapes=[
            pltpu.VMEM((BLOCKS, LAYERS, ROWS, LANES), f32),
            pltpu.VMEM((BLOCKS, LAYERS, ROWS, LANES), f32),
            pltpu.VMEM((STEPS, 3, LAYERS, ROWS, BLOCKS * LANES), jnp.bfloat16),
            pltpu.VMEM((STEPS, 2, BLOCKS, ROWS, LANES), f32),
            pltpu.VMEM((STEPS, 2, BLOCKS, ROWS, LANES), f32),
            pltpu.VMEM((STEPS, 2, CHUNKS, 2 * LAYERS, LANES), f32),
            pltpu.VMEM((STEPS, 2, CHUNKS, 2 * LAYERS, LANES), f32),
            pltpu.VMEM((STEPS, BLOCKS, ROWS, LANES), f32),
            pltpu.VMEM((BLOCKS, ROWS, LANES), f32),
            pltpu.VMEM((PROWS, LANES), f32),
            pltpu.VMEM((PROWS, LANES), jnp.int32),
            pltpu.VMEM((STEPS, PROWS, LANES), f32),
            pltpu.VMEM((PZ, PROWS, LANES), f32),
            pltpu.VMEM((PZ, PROWS, LANES), f32),
            pltpu.VMEM((STEPS, PROWS, LANES), f32),
            pltpu.VMEM((STEPS, PZ, PROWS, LANES), f32),
            pltpu.VMEM((STEPS, PZ, PROWS, LANES), jnp.int32),
            pltpu.VMEM((PZ, PROWS, LANES), f32),
            pltpu.VMEM((STEPS + 1, 2, PZ, LANES), f32),
            pltpu.VMEM((STEPS, 2, PZ, LANES), f32),
            pltpu.VMEM((STEPS + 1, 8, LANES), f32),
            pltpu.VMEM((STEPS, 2, 8, LANES), f32),
            pltpu.VMEM((LAYERS, ROWS, LANES), f32),
            pltpu.VMEM((LAYERS, ROWS, LANES), f32),
            pltpu.VMEM((STEPS, BLOCKS, ROWS, LANES), f32),
            pltpu.VMEM((STEPS, BLOCKS, ROWS, LANES), f32),
            pltpu.VMEM((PROWS, LANES), f32),
            pltpu.VMEM((BLOCKS, LAYERS, ROWS, LANES), f32),
            pltpu.VMEM((BLOCKS, LAYERS, ROWS, LANES), f32),
            pltpu.VMEM((LAYERS, ROWS, LANES), f32),
            pltpu.VMEM((LAYERS, ROWS, LANES), f32),
            pltpu.VMEM((STEPS, 2, CHUNKS, 2 * LAYERS, LANES), f32),
            pltpu.VMEM((STEPS, 2, CHUNKS, 2 * LAYERS, LANES), f32),
            dma((BLOCKS,)),
            dma((STEPS, 3)),
            dma((2,)),
            dma((STEPS, 2)),
            dma((CHUNKS + 1,)),
            dma((STEPS, 2, CHUNKS)),
            dma((STEPS, 2, CHUNKS)),
            dma((STEPS, 2, CHUNKS)),
            dma((STEPS, 2, CHUNKS)),
            dma((STEPS,)),
            dma((STEPS, CHUNKS)),
            dma((1,)),
            dma((CHUNKS,)),
            dma((STEPS, BLOCKS, 2)),
            dma((STEPS,)),
            dma((STEPS, 2)),
            dma((STEPS, 2)),
            dma((STEPS, 2)),
            dma((STEPS, 2)),
            dma((STEPS, 2)),
            dma((STEPS, 2)),
        ],
        compiler_params=pltpu.CompilerParams(
            collective_id=0, has_side_effects=True, vmem_limit_bytes=48 * 1024 * 1024
        ),
        cost_estimate=pl.CostEstimate(flops=35_000_000, bytes_accessed=11_000_000, transcendentals=0),
    )(*(pltpu.with_memory_space_constraint(a, pltpu.HBM) for a in (seed_fluid, seed_plate, velocity, enthalpy, phase, contact)))


def solution(mesh):
    return jax.shard_map(
        on_device,
        mesh=mesh,
        in_specs=(
            P("ty", "tx", None),
            P(None, "ty", "tx"),
            P(None, None, "ty", "tx", None),
            P(None, None, "ty", "tx"),
            P(None, None, "ty", "tx"),
            P("ty", "tx"),
        ),
        out_specs=(P("ty", "tx", None), P(None, "ty", "tx")),
        check_vma=False,
    )
```

```python
import jax
import jax.numpy as jnp
from jax import lax
from jax.experimental import pallas as pl
from jax.experimental.pallas import tpu as pltpu
from jax.sharding import PartitionSpec as P

MESH = pl.DeviceIdType.MESH
STEPS = 4
PZ = 16
LAYERS = 4
ROWS = 64
BLOCKS = 8
CHUNKS = 4
PROWS = 32
LANES = 128
STEP_SLOTS = ((0, 1), (1, 6), (2, 9), (3, 14))
TOP_SLOTS = ((0, 4), (1, 6), (2, 12), (3, 15))
CARRY_SLOTS = ((1, 8), (2, 11), (3, 15))
COUPLE_SLOTS = ((0, 4), (1, 8), (2, 12), (3, 15))
TOP_0, BASE_1, TOP_2, BASE_3, CONTACT, SLOPE_1, SLOPE_3 = range(7)
PLANES = 7
PASS_SLOTS = ((TOP_0, 1), (BASE_1, 4), (TOP_2, 10), (BASE_3, 13))
MORE_PASS_SLOTS = ((CONTACT, 1), (SLOPE_1, 2), (SLOPE_3, 11))
TX = 8
TY = 16


def kernel(
    seed_fluid, seed_plate, velocity, enthalpy, phase, contact,
    out_fluid, out_plate,
    F, NF, V, ZS, ZR, YS, YR, CR, RB, KP, CI, PR, PT, NP, TOP, EN, PH, SL, PYS, PYR, PXS, PXR, SXM, SXP, AS, AM, WD, CP, D, ND, DXM, DXP, DYS, DYR,
    load_f, load_v, load_p, load_e, out_sem,
    zs_sem, zr_sem, ys_sem, yr_sem, cs_sem, rb_sem, fw_sem, cr_sem, fs_sem, pr_sem,
    pys_sem, pyr_sem, pxs_sem, pxr_sem, dys_sem, dyr_sem, present,
):
    tx = lax.axis_index("tx")
    ty = lax.axis_index("ty")
    has_down, has_up = ty > 0, ty < TY - 1
    has_lo, has_hi = tx > 0, tx < TX - 1
    is_wall = ty == 0
    home_tx = ty // 2
    is_self = (tx == 0) & (ty == 0)
    parity, core = lax.rem(ty // 2, 2), lax.rem(ty, 2)
    pass_tx = 2 * (tx // 2) + parity
    away_from_pass = (pass_tx != tx) | (ty != 1)
    is_pass = ty == 1
    column, high = tx // 2, lax.rem(tx, 2)
    lane = lax.broadcasted_iota(jnp.int32, (ROWS, LANES), 1)
    row = lax.broadcasted_iota(jnp.int32, (ROWS, LANES), 0)

    def lanes(b):
        return pl.ds(pl.multiple_of(b * LANES, LANES), LANES)

    f_loads = [
        pltpu.make_async_copy(seed_fluid.at[:, :, pl.ds(b * LANES, LANES)], F.at[b], load_f.at[b])
        for b in range(BLOCKS)
    ]
    for copy in f_loads:
        copy.start()
    for c in (2, 1, 0):
        pltpu.make_async_copy(velocity.at[STEPS - 1, c], V.at[STEPS - 1, c], load_v.at[STEPS - 1, c]).start()
    contact_load = pltpu.make_async_copy(contact, CI, load_p.at[1])
    contact_load.start()
    plate_load = pltpu.make_async_copy(seed_plate, PT, load_p.at[0])
    plate_load.start()

    def late_loads(n):
        e = pltpu.make_async_copy(enthalpy.at[n], EN.at[n], load_e.at[n, 0])
        p = pltpu.make_async_copy(phase.at[n], PH.at[n], load_e.at[n, 1])
        v = [pltpu.make_async_copy(velocity.at[n, c], V.at[n, c], load_v.at[n, c]) for c in range(3)]
        return e, p, v

    barrier = pltpu.get_barrier_semaphore()

    def greet(cond, device):
        @pl.when(cond)
        def _():
            pl.semaphore_signal(barrier, inc=1, device_id=device, device_id_type=MESH)

        return jnp.where(cond, 1, 0)

    @pl.when(is_wall)
    def _():
        for c in range(TX):
            for r in range(2):
                greet((tx > 0) | (2 * c + r > 0), (c, 2 * tx + r))

    expected = jnp.where(is_self, 0, 1)

    @pl.when(is_pass)
    def _():
        for z in range(4):
            for k in range(4):
                to = (2 * column + k // 2, 4 * z + 2 * high + k % 2)
                greet((to[0] != tx) | (to[1] != ty), to)

    expected += jnp.where(away_from_pass, 1, 0)

    @pl.when(is_wall)
    def _():
        for x in range(4):
            greet(is_wall, (2 * x + high, 1))

    expected += jnp.where(is_pass, 4, 0)
    expected += greet(has_lo, (tx - 1, ty))
    expected += greet(has_hi, (tx + 1, ty))
    expected += greet(has_down, (tx, ty - 1))
    expected += greet(has_up, (tx, ty + 1))

    for n in (3, 2, 1, 0):
        e, p, v = late_loads(n)
        e.start()
        p.start()
        if n < STEPS - 1:
            for copy in v:
                copy.start()

    def remote(src, dst, send, recv, device):
        return pltpu.make_async_remote_copy(
            src_ref=src, dst_ref=dst, send_sem=send, recv_sem=recv, device_id=device, device_id_type=MESH
        )

    def z_down(s, j):
        blocks = pl.ds(2 * j, 2)
        return remote(ZS.at[s, 0, blocks], ZR.at[s, 1, blocks], zs_sem.at[0], zr_sem.at[s, 1, j], (tx, ty - 1))

    def z_up(s, j):
        blocks = pl.ds(2 * j, 2)
        return remote(ZS.at[s, 1, blocks], ZR.at[s, 0, blocks], zs_sem.at[1], zr_sem.at[s, 0, j], (tx, ty + 1))

    def y_lo(s, j):
        return remote(YS.at[s, 0, j], YR.at[s, 1, j], ys_sem.at[0], yr_sem.at[s, 1, j], (tx - 1, ty))

    def y_hi(s, j):
        return remote(YS.at[s, 1, j], YR.at[s, 0, j], ys_sem.at[1], yr_sem.at[s, 0, j], (tx + 1, ty))

    def wall_out(s, j, bb, r):
        b = 2 * j + bb
        return remote(
            AM.at[s, b, pl.ds(PROWS * r, PROWS)], PR.at[s], fs_sem.at[s], pr_sem.at[s], (b, 2 * tx + r)
        )

    def each_wall_out(s, j, act):
        for bb in range(2):
            for r in range(2):
                away = is_wall if (bb, r) != (0, 0) else is_wall & ((tx > 0) | (j > 0))

                @pl.when(away)
                def _(bb=bb, r=r):
                    act(wall_out(s, j, bb, r))

    def launch_y(s, j):
        pl.when(has_lo)(lambda: y_lo(s, j).start())
        pl.when(has_hi)(lambda: y_hi(s, j).start())

    def launch_z(s, j):
        pl.when(has_down)(lambda: z_down(s, j).start())
        pl.when(has_up)(lambda: z_up(s, j).start())

    def wall_launch(s, j):
        each_wall_out(s, j, lambda copy: copy.start())

        @pl.when(is_self & (j == 0))
        def _():
            pltpu.make_async_copy(AM.at[s, 0, pl.ds(0, PROWS)], PR.at[s], pr_sem.at[s]).start()

    def stage_z(s, j):
        n = STEPS - 1 - s
        for bb in range(2):
            b = 2 * j + bb
            g = 0.1 * F[b, 0]
            ZS[s, 0, b] = g + g * V[n, 2, 0, :, lanes(b)].astype(jnp.float32)
            g = 0.1 * F[b, LAYERS - 1]
            ZS[s, 1, b] = g - g * V[n, 2, LAYERS - 1, :, lanes(b)].astype(jnp.float32)

    def stage_y(s, j, field, out):
        n = STEPS - 1 - s
        for q in range(2 * LAYERS):
            b, l = 2 * j + q // LAYERS, q % LAYERS
            g = 0.1 * field[b, l, 0:1, :]
            v = V[n, 1, l, 0:16, lanes(b)].astype(jnp.float32)[0:1]
            out[s, 0, j, q : q + 1, :] = g + g * v
            g = 0.1 * field[b, l, ROWS - 1 : ROWS, :]
            v = V[n, 1, l, ROWS - 16 : ROWS, lanes(b)].astype(jnp.float32)[15:16]
            out[s, 1, j, q : q + 1, :] = g - g * v

    def prime(s, field, xp, xm):
        for l in range(LAYERS):
            g = 0.1 * field[0, l]
            xp[l] = pltpu.roll(g + g * V[STEPS - 1 - s, 0, l, :, lanes(0)].astype(jnp.float32), LANES - 1, 1)
            xm[l] = jnp.zeros((ROWS, LANES), jnp.float32)

    def interior(s, b, field, out, xp, xm):
        n = STEPS - 1 - s
        after = jnp.minimum(b + 1, BLOCKS - 1)
        weight = jnp.where(b < BLOCKS - 1, 0.1, 0.0)
        pending = below = None
        for l in range(LAYERS):
            f = field[b, l]
            g = 0.1 * f
            gu = g * V[n, 0, l, :, lanes(b)].astype(jnp.float32)
            gv = g * V[n, 1, l, :, lanes(b)].astype(jnp.float32)
            gw = g * V[n, 2, l, :, lanes(b)].astype(jnp.float32)
            beyond = weight * field[after, l]
            beyond = beyond + beyond * V[n, 0, l, :, lanes(after)].astype(jnp.float32)
            from_beyond = pltpu.roll(beyond, LANES - 1, 1)
            from_left = pltpu.roll(g - gu, 1, 1)
            from_above = pltpu.roll(g + gv, ROWS - 1, 0)
            from_below = pltpu.roll(g - gv, 1, 0)
            total = 0.4 * f
            total += jnp.where(lane == LANES - 1, from_beyond, xp[l])
            total += jnp.where(lane == 0, xm[l], from_left)
            total += jnp.where(row == ROWS - 1, 0.0, from_above)
            total += jnp.where(row == 0, 0.0, from_below)
            xp[l] = from_beyond
            xm[l] = from_left
            if l > 0:
                out[b, l - 1] = pending + (g + gw)
                total += below
            below = g - gw
            pending = total
        out[b, LAYERS - 1] = pending

    def finish(s, j):
        @pl.when(has_lo)
        def _():
            y_hi(s, j).wait_recv()
            for q in range(2 * LAYERS):
                b, l = 2 * j + q // LAYERS, q % LAYERS
                NF[b, l, 0:1, :] += YR[s, 0, j, q : q + 1, :]

        @pl.when(has_hi)
        def _():
            y_lo(s, j).wait_recv()
            for q in range(2 * LAYERS):
                b, l = 2 * j + q // LAYERS, q % LAYERS
                NF[b, l, ROWS - 1 : ROWS, :] += YR[s, 1, j, q : q + 1, :]

        for bb in range(2):
            for l in range(1, LAYERS - 1):
                F[2 * j + bb, l] = NF[2 * j + bb, l]

        @pl.when(has_down)
        def _():
            z_up(s, j).wait_recv()
            for bb in range(2):
                F[2 * j + bb, 0] = NF[2 * j + bb, 0] + ZR[s, 0, 2 * j + bb]

        @pl.when(has_up)
        def _():
            z_down(s, j).wait_recv()
            for bb in range(2):
                F[2 * j + bb, LAYERS - 1] = NF[2 * j + bb, LAYERS - 1] + ZR[s, 1, 2 * j + bb]

        @pl.when(ty == TY - 1)
        def _():
            for bb in range(2):
                F[2 * j + bb, LAYERS - 1] = NF[2 * j + bb, LAYERS - 1]

        @pl.when(is_wall)
        def _():
            for bb in range(2):
                F[2 * j + bb, 0] = NF[2 * j + bb, 0]

            @pl.when(s < STEPS - 1)
            def _():
                for bb in range(2):
                    AS[s + 1, 2 * j + bb] = NF[2 * j + bb, 0]

            @pl.when(s == 0)
            def _():
                for bb in range(2):
                    AM[1, 2 * j + bb] = NF[2 * j + bb, 0]

    def d_lo(s):
        return remote(DYS.at[s, 0], DYR.at[s, 1], dys_sem.at[0], dyr_sem.at[s, 1], (tx - 1, ty))

    def d_hi(s):
        return remote(DYS.at[s, 1], DYR.at[s, 0], dys_sem.at[1], dyr_sem.at[s, 0], (tx + 1, ty))

    def carry_on(s):
        prime(s, D, DXP, DXM)

        def body(b, c):
            interior(s, b, D, ND, DXP, DXM)
            return c

        lax.fori_loop(0, BLOCKS, body, 0)
        for here, copy, side, at in ((has_lo, d_hi, 0, 0), (has_hi, d_lo, 1, ROWS - 1)):
            @pl.when(here)
            def _(copy=copy, side=side, at=at):
                copy(s).wait_recv()
                for b in range(BLOCKS):
                    for l in range(LAYERS):
                        q = LAYERS * (b % 2) + l
                        ND[b, l, at : at + 1, :] += DYR[s, side, b // 2, q : q + 1, :]

        @pl.when(s == STEPS - 1)
        def _():
            def body(b, c):
                for l in range(LAYERS):
                    F[b, l] += ND[b, l]
                upper = pl.ds(1, LAYERS - 1)
                pltpu.make_async_copy(F.at[b, upper], out_fluid.at[upper, :, lanes(b)], out_sem.at[b // 2]).start()
                return c

            lax.fori_loop(0, BLOCKS, body, 0)

        @pl.when(s < STEPS - 1)
        def _():
            for b in range(BLOCKS):
                AM[s + 1, b] = AS[s + 1, b] + ND[b, 0]

            def body(j, c):
                wall_launch(s + 1, j)
                return c

            lax.fori_loop(0, CHUNKS, body, 0)

    def couple(s):
        def here(p):
            for j in range(CHUNKS):
                blocks = pl.ds(2 * j, 2)
                pltpu.make_async_copy(CR.at[p, blocks], CR.at[p, blocks], cr_sem.at[p, j]).wait()

        here(s)
        odd = lax.rem(s, 2) == 1

        @pl.when(s == 0)
        def _():
            here(CONTACT)

        @pl.when(odd)
        def _():
            slope = SLOPE_1 + s // 2
            here(slope)

            def body(b, c):
                KP[b] = CR[s, b] - CR[slope, b] * KP[b]
                return c

            lax.fori_loop(0, BLOCKS, body, 0)

        @pl.when(jnp.logical_not(odd))
        def _():
            def body(b, c):
                KP[b] = CR[s, b]
                return c

            lax.fori_loop(0, BLOCKS, body, 0)

        def body(b, c):
            wall = AS[s, b] + D[b, 0]
            coupling = CR[CONTACT, b] * (0.5 * KP[b] - 0.5 * wall)
            KP[b] = coupling

            @pl.when(s < STEPS - 1)
            def _():
                D[b, 0] = ND[b, 0] + coupling
                for l in range(1, LAYERS):
                    D[b, l] = ND[b, l]

            @pl.when(s == STEPS - 1)
            def _():
                F[b, 0] += coupling
                pltpu.make_async_copy(F.at[b, 0:1], out_fluid.at[0:1, :, lanes(b)], out_sem.at[b // 2]).start()

            return c

        lax.fori_loop(0, BLOCKS, body, 0)

        @pl.when(s < STEPS - 1)
        def _():
            def body(j, c):
                stage_y(s + 1, j, D, DYS)
                return c

            lax.fori_loop(0, CHUNKS, body, 0)
            pl.when(has_lo)(lambda: d_lo(s + 1).start())
            pl.when(has_hi)(lambda: d_hi(s + 1).start())

    def put_out(j):
        for bb in range(2):
            b = 2 * j + bb
            pltpu.make_async_copy(F.at[b], out_fluid.at[:, :, lanes(b)], out_sem.at[j]).start()


    def reply(p):
        return remote(TOP.at[p], RB.at[p, ty // 4, high, core_rows], cs_sem.at[0], rb_sem.at[p], (pass_tx, 1))

    def passed(p, z):
        return remote(
            RB.at[p, z], CR.at[p, pl.ds(2 * column, 2)], fw_sem.at[p], cr_sem.at[p, column], (2 * z + high, 0)
        )

    core_rows = pl.ds(pl.multiple_of(PROWS * core, PROWS), PROWS)

    def wall_reply(p):
        pl.when(away_from_pass)(lambda: reply(p).start())

        @pl.when(jnp.logical_not(away_from_pass))
        def _():
            pltpu.make_async_copy(TOP.at[p], RB.at[p, ty // 4, high, core_rows], rb_sem.at[p]).start()

    def pass_on(p):
        pltpu.make_async_copy(RB.at[p], RB.at[p], rb_sem.at[p]).wait()
        for z in range(4):
            passed(p, z).start()

    def py_lo(s):
        return remote(PYS.at[s, 0], PYR.at[s, 1], pys_sem.at[0], pyr_sem.at[s, 1], (tx, ty - 1))

    def py_hi(s):
        return remote(PYS.at[s, 1], PYR.at[s, 0], pys_sem.at[1], pyr_sem.at[s, 0], (tx, ty + 1))

    def px_lo(s):
        return remote(PXS.at[s], PXR.at[s, 1], pxs_sem.at[0], pxr_sem.at[s, 1], (tx - 1, ty))

    def px_hi(s):
        return remote(PXS.at[s], PXR.at[s, 0], pxs_sem.at[1], pxr_sem.at[s, 0], (tx + 1, ty))

    def plate_launch(s):
        pl.when(has_lo)(lambda: px_lo(s).start())
        pl.when(has_hi)(lambda: px_hi(s).start())
        pl.when(has_down)(lambda: py_lo(s).start())
        pl.when(has_up)(lambda: py_hi(s).start())

    small_lane = lax.broadcasted_iota(jnp.int32, (8, LANES), 1)

    def edge_rows(s, z, value):
        PYS[s, 0, z : z + 1, :] = value[0:1]
        PYS[s, 1, z : z + 1, :] = value[PROWS - 1 : PROWS]

    def edge_columns(packed, z, value):
        for k in range(PROWS // 8):
            place = 2 * (16 * k + z)
            part = pltpu.roll(value[8 * k : 8 * k + 8], place + 1, 1)
            packed = jnp.where((small_lane == place) | (small_lane == place + 1), part, packed)
        return packed

    def merge(parts):
        while len(parts) > 1:
            parts = [x + y for x, y in zip(parts[::2], parts[1::2])]
        return parts[0]

    def plate_edges(s, plate):
        parts = []
        for z in range(PZ):
            value = plate[z]
            edge_rows(s, z, value)
            parts.append(edge_columns(jnp.zeros((8, LANES), jnp.float32), z, value))
        PXS[s] = merge(parts)

    plate_lane = lax.broadcasted_iota(jnp.int32, (PROWS, LANES), 1)
    plate_row = lax.broadcasted_iota(jnp.int32, (PROWS, LANES), 0)

    def slopes_of(n):
        e, p, _ = late_loads(n)
        e.wait()
        p.wait()
        for z in range(PZ):
            saved, state = EN[n, z], PH[n, z]
            slopes = 1.0 / (1.0 + 8.0 * saved * (1.0 - saved))
            SL[z] = jnp.where(state == 0, 1.0, jnp.where(state == 2, 0.7, slopes))

    def plate_step(s):
        @pl.when(s > 0)
        def _():
            for z in range(PZ):
                PT[z] = NP[z]

        pl.when(has_lo)(lambda: px_hi(s).wait_recv())
        pl.when(has_hi)(lambda: px_lo(s).wait_recv())
        pl.when(has_down)(lambda: py_hi(s).wait_recv())
        pl.when(has_up)(lambda: py_lo(s).wait_recv())
        beside = jnp.where(
            small_lane % 2 == 0, pltpu.roll(PXR[s, 1], LANES - 1, 1), pltpu.roll(PXR[s, 0], 1, 1)
        )
        for z in range(PZ):
            value = PT[z]
            ends = [pltpu.roll(beside, LANES - 1 - 2 * (16 * k + z), 1) for k in range(PROWS // 8)]
            ends = jnp.concatenate(ends, 0)
            total = jnp.where(plate_lane == 0, ends, pltpu.roll(value, 1, 1))
            total += jnp.where(plate_lane == LANES - 1, ends, pltpu.roll(value, LANES - 1, 1))
            total += jnp.where(plate_row == 0, PYR[s, 0, z : z + 1, :], pltpu.roll(value, 1, 0))
            total += jnp.where(plate_row == PROWS - 1, PYR[s, 1, z : z + 1, :], pltpu.roll(value, PROWS - 1, 0))
            if z > 0:
                total += PT[z - 1]
            if z < PZ - 1:
                total += PT[z + 1]
            NP[z] = value + SL[z] * (0.12 * (total - 6.0 * value))

        @pl.when(lax.rem(s, 2) == 0)
        def _():
            TOP[s + 1] = NP[PZ - 1]
            wall_reply(s + 1)

    def plate_top(s):
        pltpu.make_async_copy(PR.at[s], PR.at[s], pr_sem.at[s]).wait()
        wall = PR[s] + jnp.where(s > 0, CP[...], 0.0)
        coupling = TOP[CONTACT] * (0.5 * PT[PZ - 1] - 0.5 * wall)
        CP[...] = coupling
        value = NP[PZ - 1] - SL[PZ - 1] * coupling
        NP[PZ - 1] = value

        @pl.when(s < STEPS - 1)
        def _():
            @pl.when(s == 1)
            def _():
                TOP[TOP_2] = value
                wall_reply(TOP_2)

            plate_edges(s + 1, NP)
            plate_launch(s + 1)

        @pl.when(s < STEPS - 1)
        def _():
            slopes_of(STEPS - 2 - s)

            @pl.when(s == 1)
            def _():
                TOP[SLOPE_3] = SL[PZ - 1]
                wall_reply(SLOPE_3)

        @pl.when(s == STEPS - 1)
        def _():
            pltpu.make_async_copy(NP, out_plate, out_sem.at[CHUNKS]).start()

    for absent, side in ((ty == 0, 0), (ty == TY - 1, 1)):
        @pl.when(absent)
        def _(side=side):
            for s in range(STEPS):
                PYR[s, side] = jnp.zeros((PZ, LANES), jnp.float32)

    for absent, side in ((tx == 0, 0), (tx == TX - 1, 1)):
        @pl.when(absent)
        def _(side=side):
            for s in range(STEPS):
                PXR[s, side] = jnp.zeros((8, LANES), jnp.float32)

    contact_load.wait()
    TOP[CONTACT] = CI[...].astype(jnp.float32)
    for copy in f_loads:
        copy.wait()
    for c in (2, 1, 0):
        pltpu.make_async_copy(velocity.at[STEPS - 1, c], V.at[STEPS - 1, c], load_v.at[STEPS - 1, c]).wait()

    def first_stage(j, carry):
        stage_z(0, j)
        stage_y(0, j, F, YS)
        return carry

    lax.fori_loop(0, CHUNKS, first_stage, 0)

    @pl.when(is_wall)
    def _():
        for b in range(BLOCKS):
            AS[0, b] = F[b, 0]
            AM[0, b] = F[b, 0]
            for l in range(LAYERS):
                D[b, l] = jnp.zeros((ROWS, LANES), jnp.float32)
                ND[b, l] = jnp.zeros((ROWS, LANES), jnp.float32)

    plate_load.wait()
    TOP[TOP_0] = PT[PZ - 1]
    plate_edges(0, PT)
    pl.semaphore_wait(barrier, expected)

    @pl.when(jnp.logical_not(is_self))
    def _():
        pl.semaphore_signal(present, inc=1, device_id=(home_tx, 0), device_id_type=MESH)

    wall_reply(CONTACT)
    wall_reply(TOP_0)

    def first_launch(j, carry):
        launch_y(0, j)
        launch_z(0, j)
        return carry

    lax.fori_loop(0, CHUNKS, first_launch, 0)
    plate_launch(0)

    def first_interior(b, carry):
        interior(0, b, F, NF, SXP, SXM)
        return carry

    prime(0, F, SXP, SXM)
    lax.fori_loop(0, BLOCKS // 2, first_interior, 0)
    lax.fori_loop(BLOCKS // 2, BLOCKS, first_interior, 0)
    slopes_of(STEPS - 1)
    TOP[SLOPE_1] = SL[PZ - 1]
    wall_reply(SLOPE_1)

    def at(t, slots, act):
        due, s = False, 0
        for step, place in slots:
            due, s = due | (t == place), jnp.where(t == place, step, s)
        pl.when(due)(lambda: act(s))

    def slot(t, carry):
        s, j = t // CHUNKS, lax.rem(t, CHUNKS)
        finish(s, j)

        @pl.when(s < STEPS - 1)
        def _():
            @pl.when(j == 0)
            def _():
                for copy in late_loads(STEPS - 2 - s)[2]:
                    copy.wait()

            stage_z(s + 1, j)
            launch_z(s + 1, j)
            stage_y(s + 1, j, F, YS)
            launch_y(s + 1, j)

            @pl.when(j == 0)
            def _():
                prime(s + 1, F, SXP, SXM)

            def body(b, c):
                interior(s + 1, b, F, NF, SXP, SXM)
                return c

            lax.fori_loop(jnp.maximum(2 * j - 1, 0), jnp.where(j == CHUNKS - 1, BLOCKS, 2 * j + 1), body, 0)

        pl.when((s == STEPS - 1) & (ty > 0))(lambda: put_out(j))

        @pl.when(is_pass)
        def _():
            at(t, MORE_PASS_SLOTS, pass_on)
            at(t, PASS_SLOTS, pass_on)

        @pl.when(is_wall & (t == 0))
        def _():
            pl.semaphore_wait(present, jnp.where(tx == 0, 15, 16))

            def body(j, c):
                wall_launch(0, j)
                return c

            lax.fori_loop(0, CHUNKS, body, 0)

        pl.when(is_wall & (s == 0))(lambda: wall_launch(1, j))

        @pl.when(is_wall)
        def _():
            at(t, CARRY_SLOTS, carry_on)
            at(t, COUPLE_SLOTS, couple)

        at(t, STEP_SLOTS, plate_step)
        at(t, TOP_SLOTS, plate_top)
        return carry

    lax.fori_loop(0, STEPS * CHUNKS, slot, 0)

    def all_sent(ref, semaphore):
        pltpu.make_async_copy(ref, ref, semaphore).wait()

    pl.when(away_from_pass)(lambda: all_sent(TOP, cs_sem.at[0]))
    some = pl.ds(0, STEPS)
    for there, k, z_or_y, z_or_y_sem, plate, plate_sem in (
        (has_lo, 0, YS.at[:, 0], ys_sem, PXS.at[some], pxs_sem),
        (has_hi, 1, YS.at[:, 1], ys_sem, PXS.at[some], pxs_sem),
        (has_down, 0, ZS.at[:, 0], zs_sem, PYS.at[some, 0], pys_sem),
        (has_up, 1, ZS.at[:, 1], zs_sem, PYS.at[some, 1], pys_sem),
    ):
        @pl.when(there)
        def _(k=k, z_or_y=z_or_y, z_or_y_sem=z_or_y_sem, plate=plate, plate_sem=plate_sem):
            all_sent(z_or_y, z_or_y_sem.at[k])
            all_sent(plate, plate_sem.at[k])

    for there, k in ((has_lo, 0), (has_hi, 1)):
        pl.when(is_wall & there)(lambda k=k: all_sent(DYS.at[pl.ds(1, STEPS - 1), k], dys_sem.at[k]))

    @pl.when(is_pass)
    def _():
        for p in range(PLANES):
            all_sent(RB.at[p], fw_sem.at[p])

    @pl.when(is_wall)
    def _():
        for s in range(STEPS):
            pl.when(is_self)(lambda s=s: all_sent(WD, fs_sem.at[s]))
            pl.when(jnp.logical_not(is_self))(lambda s=s: all_sent(AM.at[s], fs_sem.at[s]))

    for j in range(CHUNKS):
        pltpu.make_async_copy(F.at[pl.ds(2 * j, 2)], F.at[pl.ds(2 * j, 2)], out_sem.at[j]).wait()
    pltpu.make_async_copy(NP, out_plate, out_sem.at[CHUNKS]).wait()


def on_device(seed_fluid, seed_plate, velocity, enthalpy, phase, contact):
    f32 = jnp.float32
    dma = pltpu.SemaphoreType.DMA
    return pl.pallas_call(
        kernel,
        out_shape=(
            jax.ShapeDtypeStruct(seed_fluid.shape, f32),
            jax.ShapeDtypeStruct(seed_plate.shape, f32),
        ),
        in_specs=[pl.BlockSpec(memory_space=pl.ANY)] * 6,
        out_specs=(pl.BlockSpec(memory_space=pl.ANY),) * 2,
        scratch_shapes=[
            pltpu.VMEM((BLOCKS, LAYERS, ROWS, LANES), f32),
            pltpu.VMEM((BLOCKS, LAYERS, ROWS, LANES), f32),
            pltpu.VMEM((STEPS, 3, LAYERS, ROWS, BLOCKS * LANES), jnp.bfloat16),
            pltpu.VMEM((STEPS, 2, BLOCKS, ROWS, LANES), f32),
            pltpu.VMEM((STEPS, 2, BLOCKS, ROWS, LANES), f32),
            pltpu.VMEM((STEPS, 2, CHUNKS, 2 * LAYERS, LANES), f32),
            pltpu.VMEM((STEPS, 2, CHUNKS, 2 * LAYERS, LANES), f32),
            pltpu.VMEM((PLANES, BLOCKS, ROWS, LANES), f32),
            pltpu.VMEM((PLANES, 4, 2, ROWS, LANES), f32),
            pltpu.VMEM((BLOCKS, ROWS, LANES), f32),
            pltpu.VMEM((PROWS, LANES), jnp.int32),
            pltpu.VMEM((STEPS, PROWS, LANES), f32),
            pltpu.VMEM((PZ, PROWS, LANES), f32),
            pltpu.VMEM((PZ, PROWS, LANES), f32),
            pltpu.VMEM((PLANES, PROWS, LANES), f32),
            pltpu.VMEM((STEPS, PZ, PROWS, LANES), f32),
            pltpu.VMEM((STEPS, PZ, PROWS, LANES), jnp.int32),
            pltpu.VMEM((PZ, PROWS, LANES), f32),
            pltpu.VMEM((STEPS + 1, 2, PZ, LANES), f32),
            pltpu.VMEM((STEPS, 2, PZ, LANES), f32),
            pltpu.VMEM((STEPS + 1, 8, LANES), f32),
            pltpu.VMEM((STEPS, 2, 8, LANES), f32),
            pltpu.VMEM((LAYERS, ROWS, LANES), f32),
            pltpu.VMEM((LAYERS, ROWS, LANES), f32),
            pltpu.VMEM((STEPS, BLOCKS, ROWS, LANES), f32),
            pltpu.VMEM((STEPS, BLOCKS, ROWS, LANES), f32),
            pltpu.VMEM((2 * TX - 1, PROWS, LANES), f32),
            pltpu.VMEM((PROWS, LANES), f32),
            pltpu.VMEM((BLOCKS, LAYERS, ROWS, LANES), f32),
            pltpu.VMEM((BLOCKS, LAYERS, ROWS, LANES), f32),
            pltpu.VMEM((LAYERS, ROWS, LANES), f32),
            pltpu.VMEM((LAYERS, ROWS, LANES), f32),
            pltpu.VMEM((STEPS, 2, CHUNKS, 2 * LAYERS, LANES), f32),
            pltpu.VMEM((STEPS, 2, CHUNKS, 2 * LAYERS, LANES), f32),
            dma((BLOCKS,)),
            dma((STEPS, 3)),
            dma((2,)),
            dma((STEPS, 2)),
            dma((CHUNKS + 1,)),
            dma((2,)),
            dma((STEPS, 2, CHUNKS)),
            dma((2,)),
            dma((STEPS, 2, CHUNKS)),
            dma((1,)),
            dma((PLANES,)),
            dma((PLANES,)),
            dma((PLANES, CHUNKS)),
            dma((STEPS,)),
            dma((STEPS,)),
            dma((2,)),
            dma((STEPS, 2)),
            dma((2,)),
            dma((STEPS, 2)),
            dma((2,)),
            dma((STEPS, 2)),
            pltpu.SemaphoreType.REGULAR,
        ],
        compiler_params=pltpu.CompilerParams(
            collective_id=0, has_side_effects=True, vmem_limit_bytes=48 * 1024 * 1024
        ),
        cost_estimate=pl.CostEstimate(flops=35_000_000, bytes_accessed=11_000_000, transcendentals=0),
    )(*(pltpu.with_memory_space_constraint(a, pltpu.HBM) for a in (seed_fluid, seed_plate, velocity, enthalpy, phase, contact)))


def solution(mesh):
    return jax.shard_map(
        on_device,
        mesh=mesh,
        in_specs=(
            P("ty", "tx", None),
            P(None, "ty", "tx"),
            P(None, None, "ty", "tx", None),
            P(None, None, "ty", "tx"),
            P(None, None, "ty", "tx"),
            P("ty", "tx"),
        ),
        out_specs=(P("ty", "tx", None), P(None, "ty", "tx")),
        check_vma=False,
    )
```
